32 devices in a mesh: frame: 16 (over z, y, core), head: 2 (over x).
Axes of the slice: x: 2, y: 2, z: 4, core: 2. Of those that a mesh axis runs over, the one named last changes fastest.
Arguments:
- queries: bfloat16 [16384, 3072], P(('frame', 'head')), may hold values from -64 to 64, as said below
- key_rows: bfloat16 [16384, 3072], P(('frame', 'head')), may hold values from -64 to 64, as said below
- value_rows: bfloat16 [16384, 3072], P(('frame', 'head')), may hold values from -24 to 24
- block_mask: int32 [128, 128], replicated, may hold values from 0 to 1, as said below
Outputs:
- attended: bfloat16 [16384, 3072], P(('frame', 'head'))
The draws below stay inside these ranges and needn't reach their ends.
Inputs may be any that keep to these rules, and one draw needn't show every extreme that they name: block_mask holds 0 or 1; every query block attends to all key blocks of its own frame; for two frames two or more apart, the query blocks of one attend to exactly one key block of the other (the same one for all of them), and some query blocks may attend to none of it. queries are finite reals. `key_rows`: keys are finite reals.
All inputs are finite; a program needn't handle non-finite values.
Results may differ from the reference program's by a relative error of at most 0.0037.
Values may be sent and summed in bfloat16 or wider, within the bound.
A program may use at most 192 MiB of HBM per device.

```python
import math
import jax
import jax.numpy as jnp
from jax import lax

HEADS = 24
HDIM = 128
BLOCK = 128
BF = 8
FT = 1024
FRAMES = 16
TOKENS = 16384
NBLK = 128
WIDTH = 3072


def query_key_pair(key):
    width_all = HEADS * HDIM
    base_query = jnp.clip(jax.random.normal(jax.random.fold_in(key, 11), (TOKENS, width_all), jnp.float32) * 1.4, -8.0, 8.0)
    base_key = jnp.clip(jax.random.normal(jax.random.fold_in(key, 12), (TOKENS, width_all), jnp.float32) * 1.4, -8.0, 8.0)
    return (base_query, base_key)


def draw_queries(key, part):
    return query_key_pair(key)[0].astype(jnp.bfloat16)


def draw_key_rows(key, part):
    return query_key_pair(key)[1].astype(jnp.bfloat16)


def draw_block_mask(key, part):
    radius = jax.random.randint(jax.random.fold_in(key, 21), (FRAMES, FRAMES), 1, 4)
    anchor_table = jax.random.randint(jax.random.fold_in(key, 22), (FRAMES, FRAMES), 0, BF)
    block_index = jnp.arange(NBLK, dtype=jnp.int32)
    frame_of = block_index // BF
    place_of = block_index % BF
    distance = jnp.abs(frame_of[:, None] - frame_of[None, :])
    pair_radius = radius[frame_of[:, None], frame_of[None, :]]
    anchor = anchor_table[frame_of[:, None], frame_of[None, :]]
    block_gap = jnp.abs(place_of[:, None] - place_of[None, :])
    reach = jnp.where(distance < 4, 2, jnp.where(distance < 8, 1, 0))
    far_active = (place_of[None, :] == anchor) & (jnp.abs(place_of[:, None] - anchor) <= reach)
    active = jnp.where(distance == 0, True, jnp.where(distance == 1, block_gap <= pair_radius, far_active))
    return active.astype(jnp.int32)


def level_of(key, dims, shards, least, largest):
    level = 1.0
    for position, parts in shards:
        steps = jax.random.uniform(jax.random.fold_in(jax.random.fold_in(key, 6), position), (parts,), jnp.float32, least / len(shards), largest / len(shards))
        level = level * jnp.repeat(jnp.exp(steps), dims[position] // parts).reshape((-1,) + (1,) * (len(dims) - 1 - position))
    return level


def scatter_about(stream_key, shape, width, most, split=(), held_as=jnp.bfloat16):
    drawn = jax.random.normal(stream_key, shape, jnp.float32) * width
    if len(split) > 0:
        drawn = level_of(stream_key, shape, split, -0.22, 0.18) * drawn
    return jnp.clip(drawn, min=-most, max=most).astype(held_as)


def setup_inputs(seed: int = 0) -> dict:
    splits = jax.random.split(jax.random.key(seed), 5)
    queries = draw_queries(jax.random.fold_in(splits[4], 71), 0)
    key_rows = draw_key_rows(jax.random.fold_in(splits[4], 71), 0)
    value_rows = scatter_about(splits[2], (TOKENS, WIDTH), 4.0, 24.0, ((0, 32),))
    block_mask = draw_block_mask(jax.random.fold_in(splits[4], 71), 0)
    return dict(queries=queries, key_rows=key_rows, value_rows=value_rows, block_mask=block_mask)


def reference(queries, key_rows, value_rows, block_mask):
    row_width = HEADS * HDIM
    score_scale = 1.0 / math.sqrt(HDIM)
    mask_grid = block_mask.reshape(FRAMES, BF, FRAMES, BF)
    used_blocks = lax.optimization_barrier(jnp.max(mask_grid, axis=1))
    block_ids = jnp.arange(BF, dtype=jnp.int32)
    chosen = jnp.minimum(lax.optimization_barrier(jnp.sum(used_blocks * block_ids[None, None, :], axis=-1)), BF - 1).astype(jnp.int32)
    query_frames = queries.reshape(FRAMES, FT, row_width)
    zero_frame = jnp.zeros((1, FT, row_width), jnp.bfloat16)
    key_pad = jnp.concatenate([zero_frame, key_rows.reshape(FRAMES, FT, row_width), zero_frame], axis=0)
    value_pad = jnp.concatenate([zero_frame, value_rows.reshape(FRAMES, FT, row_width), zero_frame], axis=0)
    key_blocks = key_rows.reshape(FRAMES, BF, BLOCK, row_width)
    value_blocks = value_rows.reshape(FRAMES, BF, BLOCK, row_width)
    mask_pad = jnp.pad(mask_grid, ((0, 0), (0, 0), (1, 1), (0, 0)))
    frame_ids = jnp.arange(FRAMES, dtype=jnp.int32)

    def one_frame(frame_id):
        near_keys = lax.dynamic_slice_in_dim(key_pad, frame_id, 3, 0).reshape(3 * FT, row_width)
        near_values = lax.dynamic_slice_in_dim(value_pad, frame_id, 3, 0).reshape(3 * FT, row_width)
        picked = lax.dynamic_index_in_dim(chosen, frame_id, 0, keepdims=False)
        far_keys = key_blocks[frame_ids, picked].reshape(FRAMES * BLOCK, row_width)
        far_values = value_blocks[frame_ids, picked].reshape(FRAMES * BLOCK, row_width)
        frame_rows = lax.dynamic_index_in_dim(mask_pad, frame_id, 0, keepdims=False)
        near_mask = lax.dynamic_slice_in_dim(frame_rows, frame_id, 3, 1).reshape(BF, 3 * BF)
        own_rows = frame_rows[:, 1:-1, :]
        match = (block_ids[None, None, :] == picked[None, :, None]).astype(jnp.int32)
        far_mask = lax.optimization_barrier(jnp.sum(own_rows * match, axis=2))
        distant = (jnp.abs(frame_ids - frame_id) >= 2).astype(jnp.int32)
        far_mask = far_mask * distant[None, :]
        block_on = jnp.concatenate([near_mask, far_mask], axis=1) > 0
        token_on = jnp.repeat(jnp.repeat(block_on, BLOCK, axis=0), BLOCK, axis=1)
        all_keys = jnp.concatenate([near_keys, far_keys], axis=0)
        all_values = jnp.concatenate([near_values, far_values], axis=0)
        frame_query = lax.dynamic_index_in_dim(query_frames, frame_id, 0, keepdims=False)

        def one_head(head_no):
            head_query = lax.dynamic_slice_in_dim(frame_query, head_no * HDIM, HDIM, 1)
            head_keys = lax.dynamic_slice_in_dim(all_keys, head_no * HDIM, HDIM, 1)
            head_values = lax.dynamic_slice_in_dim(all_values, head_no * HDIM, HDIM, 1)
            scores = lax.dot_general(head_query, head_keys, (((1,), (1,)), ((), ())), preferred_element_type=jnp.float32) * score_scale
            scores = jnp.where(token_on, scores, -1e+30)
            row_top = lax.optimization_barrier(jnp.max(scores, axis=1, keepdims=True))
            weights = jnp.exp(scores - row_top)
            denominator = lax.optimization_barrier(jnp.sum(weights, axis=1, keepdims=True))
            result = jnp.dot(weights.astype(jnp.bfloat16), head_values, preferred_element_type=jnp.float32) / denominator
            return result.astype(jnp.bfloat16)
        heads = lax.map(one_head, jnp.arange(HEADS, dtype=jnp.int32))
        return jnp.transpose(heads, (1, 0, 2)).reshape(FT, row_width)
    results = lax.map(one_frame, frame_ids)
    return results.reshape(TOKENS, row_width)
```

```python
import functools
import math

import jax
import jax.numpy as jnp
from jax import lax
from jax.experimental import pallas as pl
from jax.experimental.pallas import tpu as pltpu
from jax.sharding import PartitionSpec as P

HDIM = 128
BLOCK = 128
BF = 8
MESH = pl.DeviceIdType.MESH
GROUP_HEADS = 2
TILE_BLOCKS = 2
LOG2E = 1.4426950408889634


def kernel(
    frames,
    heads_axis,
    groups,
    pick_ref,
    bias_ref,
    q_ref,
    k_ref,
    v_ref,
    out_ref,
    own,
    near,
    far,
    parcel,
    stage,
    rows,
    local_sem,
    swap_send,
    swap_recv,
    near_send,
    near_recv,
    far_send,
    far_recv,
    out_local,
    out_send,
    out_recv,
):
    f = lax.axis_index("frame")
    h = lax.axis_index("head")
    span = GROUP_HEADS * HDIM
    nb = BF // heads_axis
    sources = (k_ref, v_ref, q_ref)

    def columns(owner, g):
        return pl.ds(pl.multiple_of((owner * groups + g) * span, span), span)

    def landing(kind, g, part):
        place = pl.ds(part * nb, nb)
        return rows.at[g, place] if kind == 2 else own.at[g, kind, place]

    def swap(kind, g, shift):
        to = lax.rem(h + shift, heads_axis)
        return pltpu.make_async_remote_copy(
            src_ref=sources[kind].at[:, :, columns(to, g)],
            dst_ref=landing(kind, g, h),
            send_sem=swap_send.at[kind, g, shift - 1],
            recv_sem=swap_recv.at[kind, g, shift - 1],
            device_id=(f, to),
            device_id_type=MESH,
        )

    def swap_wait(kind, g, shift):
        start = lax.rem(h + heads_axis - shift, heads_axis)
        pltpu.make_async_remote_copy(
            src_ref=sources[kind].at[:, :, columns(h, g)],
            dst_ref=landing(kind, g, start),
            send_sem=swap_send.at[kind, g, shift - 1],
            recv_sem=swap_recv.at[kind, g, shift - 1],
            device_id=(f, start),
            device_id_type=MESH,
        ).wait_recv()

    def keep(kind, g):
        return pltpu.make_async_copy(
            sources[kind].at[:, :, columns(h, g)], landing(kind, g, h), local_sem.at[kind, g]
        )

    def near_copy(g, side):
        to = f + 1 if side == 0 else f - 1
        return pltpu.make_async_remote_copy(
            src_ref=own.at[g],
            dst_ref=near.at[g, side],
            send_sem=near_send.at[g, side],
            recv_sem=near_recv.at[g, side],
            device_id=(to, h),
            device_id_type=MESH,
        )

    def far_copy(g, to):
        return pltpu.make_async_remote_copy(
            src_ref=parcel.at[g, to],
            dst_ref=far.at[g, f],
            send_sem=far_send.at[g, to],
            recv_sem=far_recv.at[g, f],
            device_id=(to, h),
            device_id_type=MESH,
        )

    def far_wait(g, start):
        pltpu.make_async_remote_copy(
            src_ref=parcel.at[g, start],
            dst_ref=far.at[g, start],
            send_sem=far_send.at[g, start],
            recv_sem=far_recv.at[g, start],
            device_id=(start, h),
            device_id_type=MESH,
        ).wait_recv()

    def distant(other):
        return (other - f >= 2) | (f - other >= 2)

    def out_copy(g, shift):
        to = lax.rem(h + shift, heads_axis)
        return pltpu.make_async_remote_copy(
            src_ref=rows.at[g, pl.ds(to * nb, nb)],
            dst_ref=out_ref.at[:, :, columns(h, g)],
            send_sem=out_send.at[g, shift - 1],
            recv_sem=out_recv.at[g, shift - 1],
            device_id=(f, to),
            device_id_type=MESH,
        )

    def out_wait(g, shift):
        start = lax.rem(h + heads_axis - shift, heads_axis)
        pltpu.make_async_remote_copy(
            src_ref=rows.at[g, pl.ds(start * nb, nb)],
            dst_ref=out_ref.at[:, :, columns(start, g)],
            send_sem=out_send.at[g, shift - 1],
            recv_sem=out_recv.at[g, shift - 1],
            device_id=(f, start),
            device_id_type=MESH,
        ).wait_recv()

    def out_keep(g):
        return pltpu.make_async_copy(
            rows.at[g, pl.ds(h * nb, nb)], out_ref.at[:, :, columns(h, g)], out_local.at[g]
        )

    barrier = pltpu.get_barrier_semaphore()

    @pl.loop(1, frames)
    def _(step):
        pl.semaphore_signal(
            barrier, inc=1, device_id=(lax.rem(f + step, frames), h), device_id_type=MESH
        )

    for shift in range(1, heads_axis):
        pl.semaphore_signal(
            barrier,
            inc=1,
            device_id=(f, lax.rem(h + shift, heads_axis)),
            device_id_type=MESH,
        )
    pl.semaphore_wait(barrier, frames - 1 + heads_axis - 1)

    @pl.loop(0, groups)
    def _(g):
        for kind in (0, 1):
            for shift in range(1, heads_axis):
                swap(kind, g, shift).start()
            keep(kind, g).start()

    @pl.loop(0, groups)
    def _(g):
        for shift in range(1, heads_axis):
            swap(2, g, shift).start()
        keep(2, g).start()

    @pl.loop(0, groups)
    def _(g):
        @pl.loop(0, frames)
        def _(other):
            @pl.when(jnp.logical_not(distant(other)))
            def _():
                far[g, other] = jnp.zeros(far.shape[2:], far.dtype)

        @pl.when(f == 0)
        def _():
            near[g, 0] = jnp.zeros(near.shape[2:], near.dtype)

        @pl.when(f == frames - 1)
        def _():
            near[g, 1] = jnp.zeros(near.shape[2:], near.dtype)

    @pl.loop(0, groups)
    def _(g):
        for kind in (0, 1):
            keep(kind, g).wait()
            for shift in range(1, heads_axis):
                swap_wait(kind, g, shift)
            stage[kind] = own[g, kind]

        @pl.loop(1, frames)
        def _(step):
            to = lax.rem(f + step, frames)

            @pl.when(distant(to))
            def _():
                block = pick_ref[to]
                parcel[g, to, 0] = stage[0, block]
                parcel[g, to, 1] = stage[1, block]
                far_copy(g, to).start()

        @pl.when(f < frames - 1)
        def _():
            near_copy(g, 0).start()

        @pl.when(f > 0)
        def _():
            near_copy(g, 1).start()

    scale = LOG2E / math.sqrt(HDIM)
    frame_len = BF * BLOCK
    tile = TILE_BLOCKS * BLOCK

    @pl.loop(0, groups)
    def _(g):
        keep(2, g).wait()
        for shift in range(1, heads_axis):
            swap_wait(2, g, shift)

        @pl.when(f > 0)
        def _():
            near_copy(g, 0).wait_recv()

        @pl.when(f < frames - 1)
        def _():
            near_copy(g, 1).wait_recv()

        @pl.loop(1, frames)
        def _(step):
            start = lax.rem(f + step, frames)

            @pl.when(distant(start))
            def _():
                far_wait(g, start)

        @pl.loop(0, BF // TILE_BLOCKS)
        def _(t):
            for head in range(GROUP_HEADS):
                lanes = slice(head * HDIM, (head + 1) * HDIM)
                query = rows[g, pl.ds(t * TILE_BLOCKS, TILE_BLOCKS), :, lanes].reshape(tile, HDIM)

                def part(which, no):
                    if no == 0:
                        held = own[g, which, :, :, lanes]
                    elif no < 3:
                        held = near[g, no - 1, which, :, :, lanes]
                    else:
                        held = far[g, pl.ds((no - 3) * BF, BF), which, :, lanes]
                    return held.reshape(frame_len, HDIM)

                count = 3 + frames // BF
                scores = []
                top = None
                for no in range(count):
                    s = lax.dot_general(
                        query,
                        part(0, no),
                        (((1,), (1,)), ((), ())),
                        preferred_element_type=jnp.float32,
                    )
                    off = bias_ref[t, :, :, no * frame_len : (no + 1) * frame_len]
                    s = (s.reshape(TILE_BLOCKS, BLOCK, frame_len) + off).reshape(tile, frame_len)
                    part_top = jnp.max(s, axis=1, keepdims=True)
                    top = part_top if top is None else jnp.maximum(top, part_top)
                    scores.append(s)
                total = None
                summed = None
                for no in range(count):
                    weights = jnp.exp2((scores[no] - top) * scale)
                    part_total = jnp.sum(weights, axis=1, keepdims=True)
                    part_sum = jnp.dot(
                        weights.astype(jnp.bfloat16),
                        part(1, no),
                        preferred_element_type=jnp.float32,
                    )
                    total = part_total if total is None else total + part_total
                    summed = part_sum if summed is None else summed + part_sum
                result = (summed / total).astype(jnp.bfloat16)
                rows[g, pl.ds(t * TILE_BLOCKS, TILE_BLOCKS), :, lanes] = result.reshape(
                    TILE_BLOCKS, BLOCK, HDIM
                )

        for shift in range(1, heads_axis):
            out_copy(g, shift).start()
        out_keep(g).start()

    @pl.loop(0, groups)
    def _(g):
        for kind in range(3):
            for shift in range(1, heads_axis):
                swap(kind, g, shift).wait_send()

        @pl.when(f < frames - 1)
        def _():
            near_copy(g, 0).wait_send()

        @pl.when(f > 0)
        def _():
            near_copy(g, 1).wait_send()

        @pl.loop(1, frames)
        def _(step):
            to = lax.rem(f + step, frames)

            @pl.when(distant(to))
            def _():
                far_copy(g, to).wait_send()

        out_keep(g).wait()
        for shift in range(1, heads_axis):
            out_copy(g, shift).wait_send()
            out_wait(g, shift)


def body(queries, key_rows, value_rows, block_mask):
    frames = lax.axis_size("frame")
    heads_axis = lax.axis_size("head")
    frame_id = lax.axis_index("frame")
    local, width = queries.shape
    nb = local // BLOCK
    span = GROUP_HEADS * HDIM
    groups = width // heads_axis // span
    mask_grid = block_mask.reshape(frames, BF, frames, BF)
    block_ids = jnp.arange(BF, dtype=jnp.int32)
    towards = lax.dynamic_index_in_dim(mask_grid, frame_id, 2, keepdims=False)
    pick = jnp.minimum(jnp.sum(jnp.max(towards, axis=1) * block_ids[None, :], axis=1), BF - 1)
    own_rows = lax.dynamic_index_in_dim(mask_grid, frame_id, 0, keepdims=False)
    padded_rows = jnp.pad(own_rows, ((0, 0), (1, 1), (0, 0)))
    near_mask = lax.dynamic_slice_in_dim(padded_rows, frame_id, 3, 1)
    frame_ids = jnp.arange(frames, dtype=jnp.int32)
    distant = jnp.abs(frame_ids - frame_id) >= 2
    far_mask = jnp.max(own_rows, axis=2) * distant[None, :].astype(jnp.int32)
    joint = jnp.concatenate([near_mask[:, 1], near_mask[:, 0], near_mask[:, 2], far_mask], axis=1)
    bias = jnp.where(jnp.repeat(joint > 0, BLOCK, axis=1), 0.0, -1e30).astype(jnp.float32)
    bias = bias.reshape(BF // TILE_BLOCKS, TILE_BLOCKS, 1, bias.shape[1])
    folded = (nb, BLOCK, width)
    dma = pltpu.SemaphoreType.DMA
    turns = max(heads_axis - 1, 1)
    out = pl.pallas_call(
        functools.partial(kernel, frames, heads_axis, groups),
        out_shape=jax.ShapeDtypeStruct(folded, jnp.bfloat16),
        in_specs=[
            pl.BlockSpec(memory_space=pltpu.SMEM),
            pl.BlockSpec(memory_space=pltpu.VMEM),
            pl.BlockSpec(memory_space=pl.ANY),
            pl.BlockSpec(memory_space=pl.ANY),
            pl.BlockSpec(memory_space=pl.ANY),
        ],
        out_specs=pl.BlockSpec(memory_space=pl.ANY),
        scratch_shapes=[
            pltpu.VMEM((groups, 2, BF, BLOCK, span), jnp.bfloat16),
            pltpu.VMEM((groups, 2, 2, BF, BLOCK, span), jnp.bfloat16),
            pltpu.VMEM((groups, frames, 2, BLOCK, span), jnp.bfloat16),
            pltpu.VMEM((groups, frames, 2, BLOCK, span), jnp.bfloat16),
            pltpu.VMEM((2, BF, BLOCK, span), jnp.bfloat16),
            pltpu.VMEM((groups, BF, BLOCK, span), jnp.bfloat16),
            dma((3, groups)),
            dma((3, groups, turns)),
            dma((3, groups, turns)),
            dma((groups, 2)),
            dma((groups, 2)),
            dma((groups, frames)),
            dma((groups, frames)),
            dma((groups,)),
            dma((groups, turns)),
            dma((groups, turns)),
        ],
        compiler_params=pltpu.CompilerParams(
            collective_id=0, has_side_effects=True, vmem_limit_bytes=60 * 1024 * 1024
        ),
        cost_estimate=pl.CostEstimate(
            flops=4 * BF * BLOCK * bias.shape[-1] * (width // heads_axis),
            bytes_accessed=8 * local * width,
            transcendentals=BF * BLOCK * bias.shape[-1] * groups * GROUP_HEADS,
        ),
    )(
        pick.astype(jnp.int32),
        bias,
        queries.reshape(folded),
        key_rows.reshape(folded),
        value_rows.reshape(folded),
    )
    return out.reshape(local, width)


def solution(mesh):
    placed = (
        P(("frame", "head"), None),
        P(("frame", "head"), None),
        P(("frame", "head"), None),
        P(),
    )
    return jax.shard_map(
        body, mesh=mesh, in_specs=placed, out_specs=P(("frame", "head"), None), check_vma=False
    )
```

```python
import functools
import math

import jax
import jax.numpy as jnp
from jax import lax
from jax.experimental import pallas as pl
from jax.experimental.pallas import tpu as pltpu
from jax.sharding import PartitionSpec as P

HDIM = 128
BLOCK = 128
BF = 8
MESH = pl.DeviceIdType.MESH
GROUP_HEADS = 1
TILE_BLOCKS = 2
LOG2E = 1.4426950408889634


def kernel(
    frames,
    heads_axis,
    groups,
    pick_ref,
    bias_ref,
    q_ref,
    k_ref,
    v_ref,
    out_ref,
    own,
    near,
    far,
    parcel,
    stage,
    rows,
    local_sem,
    swap_send,
    swap_recv,
    near_send,
    near_recv,
    far_send,
    far_recv,
    out_local,
    out_send,
    out_recv,
):
    f = lax.axis_index("frame")
    h = lax.axis_index("head")
    span = GROUP_HEADS * HDIM
    nb = BF // heads_axis
    sources = (k_ref, v_ref, q_ref)

    def columns(owner, g):
        return pl.ds(pl.multiple_of((owner * groups + g) * span, span), span)

    def landing(kind, g, part):
        place = pl.ds(part * nb, nb)
        return rows.at[g, place] if kind == 2 else own.at[g, kind, place]

    def swap(kind, g, shift):
        to = lax.rem(h + shift, heads_axis)
        return pltpu.make_async_remote_copy(
            src_ref=sources[kind].at[:, :, columns(to, g)],
            dst_ref=landing(kind, g, h),
            send_sem=swap_send.at[kind, g, shift - 1],
            recv_sem=swap_recv.at[kind, g, shift - 1],
            device_id=(f, to),
            device_id_type=MESH,
        )

    def swap_wait(kind, g, shift):
        start = lax.rem(h + heads_axis - shift, heads_axis)
        pltpu.make_async_remote_copy(
            src_ref=sources[kind].at[:, :, columns(h, g)],
            dst_ref=landing(kind, g, start),
            send_sem=swap_send.at[kind, g, shift - 1],
            recv_sem=swap_recv.at[kind, g, shift - 1],
            device_id=(f, start),
            device_id_type=MESH,
        ).wait_recv()

    def keep(kind, g):
        return pltpu.make_async_copy(
            sources[kind].at[:, :, columns(h, g)], landing(kind, g, h), local_sem.at[kind, g]
        )

    def near_copy(g, side):
        to = f + 1 if side == 0 else f - 1
        return pltpu.make_async_remote_copy(
            src_ref=own.at[g],
            dst_ref=near.at[g, side],
            send_sem=near_send.at[g, side],
            recv_sem=near_recv.at[g, side],
            device_id=(to, h),
            device_id_type=MESH,
        )

    def far_copy(g, to):
        return pltpu.make_async_remote_copy(
            src_ref=parcel.at[g, to],
            dst_ref=far.at[g, f],
            send_sem=far_send.at[g, to],
            recv_sem=far_recv.at[g, f],
            device_id=(to, h),
            device_id_type=MESH,
        )

    def far_wait(g, start):
        pltpu.make_async_remote_copy(
            src_ref=parcel.at[g, start],
            dst_ref=far.at[g, start],
            send_sem=far_send.at[g, start],
            recv_sem=far_recv.at[g, start],
            device_id=(start, h),
            device_id_type=MESH,
        ).wait_recv()

    def distant(other):
        return (other - f >= 2) | (f - other >= 2)

    def out_copy(g, shift):
        to = lax.rem(h + shift, heads_axis)
        return pltpu.make_async_remote_copy(
            src_ref=rows.at[g, pl.ds(to * nb, nb)],
            dst_ref=out_ref.at[:, :, columns(h, g)],
            send_sem=out_send.at[g, shift - 1],
            recv_sem=out_recv.at[g, shift - 1],
            device_id=(f, to),
            device_id_type=MESH,
        )

    def out_wait(g, shift):
        start = lax.rem(h + heads_axis - shift, heads_axis)
        pltpu.make_async_remote_copy(
            src_ref=rows.at[g, pl.ds(start * nb, nb)],
            dst_ref=out_ref.at[:, :, columns(start, g)],
            send_sem=out_send.at[g, shift - 1],
            recv_sem=out_recv.at[g, shift - 1],
            device_id=(f, start),
            device_id_type=MESH,
        ).wait_recv()

    def out_keep(g):
        return pltpu.make_async_copy(
            rows.at[g, pl.ds(h * nb, nb)], out_ref.at[:, :, columns(h, g)], out_local.at[g]
        )

    barrier = pltpu.get_barrier_semaphore()

    @pl.loop(1, frames)
    def _(step):
        pl.semaphore_signal(
            barrier, inc=1, device_id=(lax.rem(f + step, frames), h), device_id_type=MESH
        )

    for shift in range(1, heads_axis):
        pl.semaphore_signal(
            barrier,
            inc=1,
            device_id=(f, lax.rem(h + shift, heads_axis)),
            device_id_type=MESH,
        )
    pl.semaphore_wait(barrier, frames - 1 + heads_axis - 1)

    @pl.loop(0, groups)
    def _(g):
        for kind in (0, 1):
            for shift in range(1, heads_axis):
                swap(kind, g, shift).start()
            keep(kind, g).start()

    @pl.loop(0, groups)
    def _(g):
        for shift in range(1, heads_axis):
            swap(2, g, shift).start()
        keep(2, g).start()

    @pl.loop(0, groups)
    def _(g):
        @pl.loop(0, frames)
        def _(other):
            @pl.when(jnp.logical_not(distant(other)))
            def _():
                far[g, other] = jnp.zeros(far.shape[2:], far.dtype)

        @pl.when(f == 0)
        def _():
            near[g, 0] = jnp.zeros(near.shape[2:], near.dtype)

        @pl.when(f == frames - 1)
        def _():
            near[g, 1] = jnp.zeros(near.shape[2:], near.dtype)

    @pl.loop(0, groups)
    def _(g):
        for kind in (0, 1):
            keep(kind, g).wait()
            for shift in range(1, heads_axis):
                swap_wait(kind, g, shift)
            stage[kind] = own[g, kind]

        @pl.loop(1, frames)
        def _(step):
            to = lax.rem(f + step, frames)

            @pl.when(distant(to))
            def _():
                block = pick_ref[to]
                parcel[g, to, 0] = stage[0, block]
                parcel[g, to, 1] = stage[1, block]
                far_copy(g, to).start()

        @pl.when(f < frames - 1)
        def _():
            near_copy(g, 0).start()

        @pl.when(f > 0)
        def _():
            near_copy(g, 1).start()

    scale = LOG2E / math.sqrt(HDIM)
    frame_len = BF * BLOCK
    tile = TILE_BLOCKS * BLOCK

    @pl.loop(0, groups)
    def _(g):
        keep(2, g).wait()
        for shift in range(1, heads_axis):
            swap_wait(2, g, shift)

        @pl.when(f > 0)
        def _():
            near_copy(g, 0).wait_recv()

        @pl.when(f < frames - 1)
        def _():
            near_copy(g, 1).wait_recv()

        @pl.loop(1, frames)
        def _(step):
            start = lax.rem(f + step, frames)

            @pl.when(distant(start))
            def _():
                far_wait(g, start)

        @pl.loop(0, BF // TILE_BLOCKS)
        def _(t):
            for head in range(GROUP_HEADS):
                lanes = slice(head * HDIM, (head + 1) * HDIM)
                query = rows[g, pl.ds(t * TILE_BLOCKS, TILE_BLOCKS), :, lanes].reshape(tile, HDIM)

                def part(which, no):
                    if no == 0:
                        held = own[g, which, :, :, lanes]
                    elif no < 3:
                        held = near[g, no - 1, which, :, :, lanes]
                    else:
                        held = far[g, pl.ds((no - 3) * BF, BF), which, :, lanes]
                    return held.reshape(frame_len, HDIM)

                count = 3 + frames // BF
                scores = []
                top = None
                for no in range(count):
                    s = lax.dot_general(
                        query,
                        part(0, no),
                        (((1,), (1,)), ((), ())),
                        preferred_element_type=jnp.float32,
                    )
                    off = bias_ref[t, :, :, no * frame_len : (no + 1) * frame_len]
                    s = (s.reshape(TILE_BLOCKS, BLOCK, frame_len) + off).reshape(tile, frame_len)
                    part_top = jnp.max(s, axis=1, keepdims=True)
                    top = part_top if top is None else jnp.maximum(top, part_top)
                    scores.append(s)
                total = None
                summed = None
                for no in range(count):
                    weights = jnp.exp2((scores[no] - top) * scale)
                    part_total = jnp.sum(weights, axis=1, keepdims=True)
                    part_sum = jnp.dot(
                        weights.astype(jnp.bfloat16),
                        part(1, no),
                        preferred_element_type=jnp.float32,
                    )
                    total = part_total if total is None else total + part_total
                    summed = part_sum if summed is None else summed + part_sum
                result = (summed / total).astype(jnp.bfloat16)
                rows[g, pl.ds(t * TILE_BLOCKS, TILE_BLOCKS), :, lanes] = result.reshape(
                    TILE_BLOCKS, BLOCK, HDIM
                )

        for shift in range(1, heads_axis):
            out_copy(g, shift).start()
        out_keep(g).start()

    @pl.loop(0, groups)
    def _(g):
        for kind in range(3):
            for shift in range(1, heads_axis):
                swap(kind, g, shift).wait_send()

        @pl.when(f < frames - 1)
        def _():
            near_copy(g, 0).wait_send()

        @pl.when(f > 0)
        def _():
            near_copy(g, 1).wait_send()

        @pl.loop(1, frames)
        def _(step):
            to = lax.rem(f + step, frames)

            @pl.when(distant(to))
            def _():
                far_copy(g, to).wait_send()

        out_keep(g).wait()
        for shift in range(1, heads_axis):
            out_copy(g, shift).wait_send()
            out_wait(g, shift)


def body(queries, key_rows, value_rows, block_mask):
    frames = lax.axis_size("frame")
    heads_axis = lax.axis_size("head")
    frame_id = lax.axis_index("frame")
    local, width = queries.shape
    nb = local // BLOCK
    span = GROUP_HEADS * HDIM
    groups = width // heads_axis // span
    mask_grid = block_mask.reshape(frames, BF, frames, BF)
    block_ids = jnp.arange(BF, dtype=jnp.int32)
    towards = lax.dynamic_index_in_dim(mask_grid, frame_id, 2, keepdims=False)
    pick = jnp.minimum(jnp.sum(jnp.max(towards, axis=1) * block_ids[None, :], axis=1), BF - 1)
    own_rows = lax.dynamic_index_in_dim(mask_grid, frame_id, 0, keepdims=False)
    padded_rows = jnp.pad(own_rows, ((0, 0), (1, 1), (0, 0)))
    near_mask = lax.dynamic_slice_in_dim(padded_rows, frame_id, 3, 1)
    frame_ids = jnp.arange(frames, dtype=jnp.int32)
    distant = jnp.abs(frame_ids - frame_id) >= 2
    far_mask = jnp.max(own_rows, axis=2) * distant[None, :].astype(jnp.int32)
    joint = jnp.concatenate([near_mask[:, 1], near_mask[:, 0], near_mask[:, 2], far_mask], axis=1)
    bias = jnp.where(jnp.repeat(joint > 0, BLOCK, axis=1), 0.0, -1e30).astype(jnp.float32)
    bias = bias.reshape(BF // TILE_BLOCKS, TILE_BLOCKS, 1, bias.shape[1])
    folded = (nb, BLOCK, width)
    dma = pltpu.SemaphoreType.DMA
    turns = max(heads_axis - 1, 1)
    out = pl.pallas_call(
        functools.partial(kernel, frames, heads_axis, groups),
        out_shape=jax.ShapeDtypeStruct(folded, jnp.bfloat16),
        in_specs=[
            pl.BlockSpec(memory_space=pltpu.SMEM),
            pl.BlockSpec(memory_space=pltpu.VMEM),
            pl.BlockSpec(memory_space=pl.ANY),
            pl.BlockSpec(memory_space=pl.ANY),
            pl.BlockSpec(memory_space=pl.ANY),
        ],
        out_specs=pl.BlockSpec(memory_space=pl.ANY),
        scratch_shapes=[
            pltpu.VMEM((groups, 2, BF, BLOCK, span), jnp.bfloat16),
            pltpu.VMEM((groups, 2, 2, BF, BLOCK, span), jnp.bfloat16),
            pltpu.VMEM((groups, frames, 2, BLOCK, span), jnp.bfloat16),
            pltpu.VMEM((groups, frames, 2, BLOCK, span), jnp.bfloat16),
            pltpu.VMEM((2, BF, BLOCK, span), jnp.bfloat16),
            pltpu.VMEM((groups, BF, BLOCK, span), jnp.bfloat16),
            dma((3, groups)),
            dma((3, groups, turns)),
            dma((3, groups, turns)),
            dma((groups, 2)),
            dma((groups, 2)),
            dma((groups, frames)),
            dma((groups, frames)),
            dma((groups,)),
            dma((groups, turns)),
            dma((groups, turns)),
        ],
        compiler_params=pltpu.CompilerParams(
            collective_id=0, has_side_effects=True, vmem_limit_bytes=60 * 1024 * 1024
        ),
        cost_estimate=pl.CostEstimate(
            flops=4 * BF * BLOCK * bias.shape[-1] * (width // heads_axis),
            bytes_accessed=8 * local * width,
            transcendentals=BF * BLOCK * bias.shape[-1] * groups * GROUP_HEADS,
        ),
    )(
        pick.astype(jnp.int32),
        bias,
        queries.reshape(folded),
        key_rows.reshape(folded),
        value_rows.reshape(folded),
    )
    return out.reshape(local, width)


def solution(mesh):
    placed = (
        P(("frame", "head"), None),
        P(("frame", "head"), None),
        P(("frame", "head"), None),
        P(),
    )
    return jax.shard_map(
        body, mesh=mesh, in_specs=placed, out_specs=P(("frame", "head"), None), check_vma=False
    )
```
